32 devices in a mesh: groups: 2 (over x), tensor: 16 (over z, y, core).
Axes of the slice: x: 2, y: 2, z: 4, core: 2. Of those that a mesh axis runs over, the one named last changes fastest.
Arguments:
- queries: bfloat16 [64, 8192], P(('groups', 'tensor')), parts along dimension 0, may hold values from -5 to 5
- key_value_cache: bfloat16 [64, 512, 2, 1024], P(('groups', 'tensor')), parts along dimension 0, may hold values from -5 to 5
- live_cache_length: int32 [64], P(('groups', 'tensor')), parts along dimension 0, may hold values from 2 to 512
- residual: bfloat16 [64, 8192], P(('groups', 'tensor')), parts along dimension 0, may hold values from -2 to 2
- row_adapter_index: int32 [64, 1], P(('groups', 'tensor')), parts along dimension 0, may hold values from 0 to 15
- adapter_slot_index: int32 [16], replicated, may hold values from 0 to 15, each once
- output_projection_weight: bfloat16 [8192, 8192], P('tensor'), may hold values from -0.0625 to 0.0625
- adapter_down_weight: bfloat16 [16, 16, 8192], P('tensor'), may hold values from -0.0625 to 0.0625
- adapter_up_weight: bfloat16 [16, 16, 8192], P('tensor'), may hold values from -0.75 to 0.75
- norm_gain_weight: float32 [8192], replicated, may hold values from 0.5 to 1.5
Outputs:
- hidden: bfloat16 [64, 8192], P(('groups', 'tensor')), parts along dimension 0
- normed: bfloat16 [64, 8192], P(('groups', 'tensor')), parts along dimension 0
The draws below stay inside these ranges and needn't reach their ends.
There are 2 independent parts, one for each index of `groups`. The reference program is written for one: setup_inputs(seed, part) draws one part's arguments, and reference() takes and returns one part's arrays. A program takes and returns all parts, laid end to end along the dimension named above; an argument that names none is the same for every part. Nothing has to cross between parts.
Inputs may be any that keep to these rules, and one draw needn't show every extreme that they name: `row_adapter_index`: every adapter is named by at least one row. `adapter_slot_index`: each slot holds exactly one adapter.
All inputs are finite; a program needn't handle non-finite values.
Results may differ from the reference program's by a relative error of at most 0.007.
Values may be sent and summed in bfloat16 or wider, within the bound.
A program may use at most 64 MiB of HBM per device.

```python
import math
import jax
import jax.numpy as jnp
from jax import lax

MODEL_WIDTH = 8192
HQ = 64
KEY_HEADS = 8
HEAD_SIZE = 128
ADAPTER_RANK = 16
CACHE_SLOTS = 512
HEADS_PER_GROUP = 8
ATTENTION_WIDTH = 8192
DECODE_ROWS = 32
ADAPTER_COUNT = 16


def draw_key_value_cache(key, part):
    key = jax.random.fold_in(key, 31)
    output_result = jnp.clip(jax.random.normal(key, (DECODE_ROWS, CACHE_SLOTS, 2, KEY_HEADS * HEAD_SIZE), jnp.float32), -5.0, 5.0)
    return output_result.astype(jnp.bfloat16)


def draw_queries(key, part):
    key = jax.random.fold_in(key, 32)
    first_random_key = jax.random.fold_in(key, 0)
    output_result = jnp.clip(jax.random.normal(first_random_key, (DECODE_ROWS, KEY_HEADS, HEADS_PER_GROUP, HEAD_SIZE), jnp.float32), -5.0, 5.0)
    return output_result.reshape(DECODE_ROWS, KEY_HEADS * HEADS_PER_GROUP * HEAD_SIZE).astype(jnp.bfloat16)


def draw_live_cache_length(key, part):
    key = jax.random.fold_in(key, 33)
    first_random_key, second_random_key, third_random_key, key_four = jax.random.split(key, 4)
    longer = jax.random.randint(first_random_key, (DECODE_ROWS,), 2, CACHE_SLOTS + 1)
    shorter = jax.random.randint(second_random_key, (DECODE_ROWS,), 2, CACHE_SLOTS // 4 + 1)
    long_pick = jax.random.randint(third_random_key, (DECODE_ROWS,), 0, 4) == 0
    length_rows = jnp.where(long_pick, longer, shorter)
    full_row = jax.random.randint(key_four, (), 0, DECODE_ROWS)
    return length_rows.at[full_row].set(CACHE_SLOTS).astype(jnp.int32)


def steps_of(own_key, dims, cuts, smallest, high):
    factor_of = 1.0
    for position, shards_of in cuts:
        draws = jax.random.uniform(jax.random.fold_in(jax.random.fold_in(own_key, 6), position), (shards_of,), jnp.float32, smallest / len(cuts), high / len(cuts))
        factor_of = factor_of * jnp.repeat(jnp.exp(draws), dims[position] // shards_of).reshape((-1,) + (1,) * (len(dims) - 1 - position))
    return factor_of


def choose_distinct(key, rows, number_of, top, lift):
    ranking = jax.random.permutation(jax.random.fold_in(key, 1), number_of)
    favour = ranking
    for power in range(3):
        favour = favour * favour // number_of
    favour = favour * lift // number_of
    chance = jax.random.randint(jax.random.fold_in(key, 2), (rows, number_of), 0, 4096) + favour
    fixed_rows = jax.random.permutation(jax.random.fold_in(key, 3), rows)[jnp.arange(number_of) % rows]
    chance = jnp.where(jnp.arange(rows)[:, None] == fixed_rows[None, :], 1 << 14, chance)
    score = chance * number_of + jnp.arange(number_of)
    return lax.top_k(score.astype(jnp.int32), top)[1].astype(jnp.int32)


def normal_values(rng, extent, spread, bound, pieces=(), held_as=jnp.bfloat16):
    entries = spread * jax.random.normal(rng, extent, jnp.float32)
    if pieces:
        entries = entries * steps_of(rng, extent, pieces, -0.22, 0.18)
    return jnp.clip(entries, -bound, bound).astype(held_as)


def setup_inputs(seed: int = 0, part: int = 0) -> dict:
    streams_of = jax.random.split(jax.random.key(seed), 11)
    part_splits = jax.random.split(jax.random.fold_in(streams_of[10], part), 11)
    queries = draw_queries(jax.random.fold_in(jax.random.fold_in(streams_of[10], part), 71), part)
    key_value_cache = draw_key_value_cache(jax.random.fold_in(jax.random.fold_in(streams_of[10], part), 71), part)
    live_cache_length = draw_live_cache_length(jax.random.fold_in(jax.random.fold_in(streams_of[10], part), 71), part)
    residual = normal_values(part_splits[3], (DECODE_ROWS, MODEL_WIDTH), 0.3, 2.0, ((0, 16),))
    row_adapter_index = choose_distinct(part_splits[4], DECODE_ROWS, ADAPTER_COUNT, 1, 1024)
    adapter_slot_index = jax.random.permutation(streams_of[5], ADAPTER_COUNT).astype(jnp.int32)
    output_projection_weight = normal_values(streams_of[6], (ATTENTION_WIDTH, MODEL_WIDTH), ATTENTION_WIDTH ** -0.5, 0.0625, ((0, 16),))
    adapter_down_weight = normal_values(streams_of[7], (ADAPTER_COUNT, ADAPTER_RANK, ATTENTION_WIDTH), ATTENTION_WIDTH ** -0.5, 0.0625, ((0, 16),))
    adapter_up_weight = normal_values(streams_of[8], (ADAPTER_COUNT, ADAPTER_RANK, MODEL_WIDTH), (4 * ADAPTER_RANK) ** -0.5, 0.75, ((0, 16),))
    norm_gain_weight = jnp.clip(1.0 + 0.1 * jax.random.normal(streams_of[9], (MODEL_WIDTH,), jnp.float32), 0.5, 1.5)
    return {"queries": queries, "key_value_cache": key_value_cache, "live_cache_length": live_cache_length, "residual": residual, "row_adapter_index": row_adapter_index, "adapter_slot_index": adapter_slot_index, "output_projection_weight": output_projection_weight, "adapter_down_weight": adapter_down_weight, "adapter_up_weight": adapter_up_weight, "norm_gain_weight": norm_gain_weight}


adapter_scale = 2.0
norm_eps = 1e-05
masked_score = -1e+30

def attend_row(row_of_query, row_of_cache, length_row):
    heads_of_query = row_of_query.reshape(KEY_HEADS, HEADS_PER_GROUP, HEAD_SIZE).astype(jnp.float32)
    block_of_keys = row_of_cache[:, 0, :].reshape(CACHE_SLOTS, KEY_HEADS, HEAD_SIZE).astype(jnp.float32)
    block_of_values = row_of_cache[:, 1, :].reshape(CACHE_SLOTS, KEY_HEADS, HEAD_SIZE).astype(jnp.float32)
    scores = jnp.einsum('hgd,chd->hgc', heads_of_query, block_of_keys) * (1.0 / math.sqrt(HEAD_SIZE))
    live_mask = jnp.arange(CACHE_SLOTS, dtype=jnp.int32) < length_row
    scores = jnp.where(live_mask, scores, masked_score)
    top_score = lax.optimization_barrier(jnp.max(scores, axis=-1, keepdims=True))
    weights_raw = jnp.where(live_mask, jnp.exp(scores - top_score), 0.0)
    weights_low = (weights_raw / lax.optimization_barrier(jnp.sum(weights_raw, axis=-1, keepdims=True))).astype(jnp.bfloat16)
    mixture_row = jnp.einsum('hgc,chd->hgd', weights_low.astype(jnp.float32), block_of_values)
    return mixture_row.astype(jnp.bfloat16).reshape(HQ * HEAD_SIZE)

def reference(queries, key_value_cache, live_cache_length, residual, row_adapter_index, adapter_slot_index, output_projection_weight, adapter_down_weight, adapter_up_weight, norm_gain_weight):
    mixed = lax.map(lambda triple: attend_row(triple[0], triple[1], triple[2]), (queries, key_value_cache, live_cache_length))
    base = jnp.dot(mixed, output_projection_weight, preferred_element_type=jnp.float32)
    slot_index = adapter_slot_index[row_adapter_index[:, 0]].astype(jnp.int32)

    def adapt_row(pair):
        mixture_row, single_slot = pair
        shrink_factor = jnp.dot(adapter_down_weight[single_slot], mixture_row, preferred_element_type=jnp.float32).astype(jnp.bfloat16)
        return (adapter_scale * jnp.dot(shrink_factor, adapter_up_weight[single_slot], preferred_element_type=jnp.float32)).astype(jnp.bfloat16)
    delta_rows = lax.map(adapt_row, (mixed, slot_index))
    hidden_sum = residual.astype(jnp.float32) + base + delta_rows.astype(jnp.float32)
    mean_square = lax.optimization_barrier(jnp.mean(hidden_sum * hidden_sum, axis=-1, keepdims=True))
    normed = hidden_sum * lax.rsqrt(mean_square + norm_eps) * norm_gain_weight
    return (hidden_sum.astype(jnp.bfloat16), normed.astype(jnp.bfloat16))
```

```python
import functools
import math

import jax
import jax.numpy as jnp
from jax import lax
from jax.experimental import pallas as pl
from jax.experimental.pallas import tpu as pltpu
from jax.sharding import PartitionSpec as P

HQ = 64
KEY_HEADS = 8
HEAD_SIZE = 128
HEADS_PER_GROUP = 8


adapter_scale = 2.0
norm_eps = 1e-05
masked_score = -1e30


def attend(queries, key_value_cache, live_cache_length):
    count_of_rows = queries.shape[0]
    cache_capacity = key_value_cache.shape[1]
    heads_of_query = queries.reshape(count_of_rows, KEY_HEADS, HEADS_PER_GROUP, HEAD_SIZE)
    block_of_keys = key_value_cache[:, :, 0, :].reshape(
        count_of_rows, cache_capacity, KEY_HEADS, HEAD_SIZE
    )
    block_of_values = key_value_cache[:, :, 1, :].reshape(
        count_of_rows, cache_capacity, KEY_HEADS, HEAD_SIZE
    )
    scores = jnp.einsum(
        "rhgd,rchd->rhgc", heads_of_query, block_of_keys, preferred_element_type=jnp.float32
    )
    scores = scores * (1.0 / math.sqrt(HEAD_SIZE))
    live_mask = (jnp.arange(cache_capacity, dtype=jnp.int32)[None, :] < live_cache_length[:, None])[
        :, None, None, :
    ]
    scores = jnp.where(live_mask, scores, masked_score)
    top_score = jnp.max(scores, axis=-1, keepdims=True)
    weights_raw = jnp.where(live_mask, jnp.exp(scores - top_score), 0.0)
    weights_low = (weights_raw / jnp.sum(weights_raw, axis=-1, keepdims=True)).astype(jnp.bfloat16)
    mixed = jnp.einsum(
        "rhgc,rchd->rhgd", weights_low, block_of_values, preferred_element_type=jnp.float32
    )
    return mixed.astype(jnp.bfloat16).reshape(count_of_rows, HQ * HEAD_SIZE)


def rows_to_shrink(tile_of_rows, selector, adapter_down_weight):
    shrink_factor = jnp.einsum(
        "dz,gz->dg", tile_of_rows, adapter_down_weight[0], preferred_element_type=jnp.float32
    )
    return (shrink_factor * selector).astype(jnp.bfloat16)


def shards(
    queries,
    key_value_cache,
    live_cache_length,
    residual,
    row_adapter_index,
    adapter_slot_index,
    output_projection_weight,
    adapter_down_weight,
    adapter_up_weight,
    norm_gain_weight,
):
    device_count = lax.axis_size("tensor")
    my_index = lax.axis_index("tensor")
    mixed = attend(queries, key_value_cache, live_cache_length)
    slot_hot = (
        row_adapter_index == jnp.arange(adapter_slot_index.shape[0], dtype=jnp.int32)[None, :]
    )
    owner_index = jnp.sum(jnp.where(slot_hot, adapter_slot_index[None, :], 0), axis=1)
    owner_hot = owner_index[:, None] == jnp.arange(device_count, dtype=jnp.int32)[None, :]
    gathered_rows, mark_rows = (
        lax.all_gather(mixed, "tensor", axis=0, tiled=True),
        lax.all_gather(owner_hot.astype(jnp.bfloat16), "tensor", axis=0, tiled=True),
    )
    owned_row_marks = lax.dynamic_slice_in_dim(mark_rows, my_index, 1, 1).astype(jnp.float32)
    width = output_projection_weight.shape[0]
    features = lax.dynamic_slice_in_dim(gathered_rows, my_index * width, width, 1)
    base_tile = jnp.dot(features, output_projection_weight, preferred_element_type=jnp.float32)
    shrink_factor = rows_to_shrink(gathered_rows, owned_row_marks, adapter_down_weight)
    delta_tile = (
        adapter_scale
        * jnp.dot(shrink_factor, adapter_up_weight[0], preferred_element_type=jnp.float32)
    ).astype(jnp.bfloat16)
    projected = lax.psum_scatter(
        base_tile + delta_tile.astype(jnp.float32), "tensor", scatter_dimension=0, tiled=True
    )
    hidden_sum = residual.astype(jnp.float32) + projected
    mean_square = jnp.mean(hidden_sum * hidden_sum, axis=-1, keepdims=True)
    normed = hidden_sum * lax.rsqrt(mean_square + norm_eps) * norm_gain_weight
    return (hidden_sum.astype(jnp.bfloat16), normed.astype(jnp.bfloat16))


CHUNKS = 4
LANES = 128


def remote(source, target, send_sem, recv_sem, peer):
    return pltpu.make_async_remote_copy(
        src_ref=source,
        dst_ref=target,
        send_sem=send_sem,
        recv_sem=recv_sem,
        device_id={"tensor": peer},
        device_id_type=pl.DeviceIdType.MESH,
    )


def fused(
    count,
    depth,
    q_ref,
    cache_ref,
    live_ref,
    residual_ref,
    row_adapter_ref,
    slot_ref,
    weight_ref,
    down_ref,
    up_ref,
    gain_ref,
    hidden_ref,
    normed_ref,
    cache,
    weight,
    message,
    arrived,
    features,
    down,
    shrink_out,
    shrink_in,
    part,
    core_in,
    y_out,
    y_in,
    z_out,
    z_in,
    total,
    cache_sem,
    weight_sem,
    message_send,
    message_recv,
    down_send,
    down_recv,
    down_local,
    shrink_send,
    shrink_recv,
    core_send,
    core_recv,
    y_send,
    y_recv,
    z_send,
    z_recv,
):
    me = lax.axis_index("tensor")
    my_core = me % 2
    my_y = (me // 2) % 2
    my_z = me // 4
    core_peer = me + 1 - 2 * my_core
    y_peer = me + 2 - 4 * my_y
    row_count = 2 * count
    columns = weight_ref.shape[1] // CHUNKS

    cache_copies = [
        pltpu.make_async_copy(cache_ref.at[b], cache.at[b], cache_sem.at[b]) for b in range(2)
    ]
    weight_copies = [
        pltpu.make_async_copy(
            weight_ref.at[:, pl.ds(j * columns, columns)], weight.at[j], weight_sem.at[j]
        )
        for j in range(CHUNKS)
    ]
    for copy in cache_copies + weight_copies:
        copy.start()

    barrier = pltpu.get_barrier_semaphore()

    @pl.loop(1, count)
    def _(step):
        pl.semaphore_signal(
            barrier,
            inc=1,
            device_id={"tensor": (me + step) % count},
            device_id_type=pl.DeviceIdType.MESH,
        )

    pl.semaphore_wait(barrier, count - 1)

    def down_copy(peer, source):
        return remote(
            down_ref.at[0, :, pl.ds(pl.multiple_of(peer * depth, depth), depth)],
            down.at[source],
            down_send.at[peer],
            down_recv.at[source],
            peer,
        )

    @pl.loop(1, count)
    def _(step):
        down_copy((me + step) % count, me).start()

    own_down = pltpu.make_async_copy(
        down_ref.at[0, :, pl.ds(pl.multiple_of(me * depth, depth), depth)],
        down.at[me],
        down_local.at[0],
    )
    own_down.start()

    adapters = slot_ref.shape[1]
    named = lax.broadcasted_iota(jnp.int32, (2, adapters), 1) == row_adapter_ref[...]
    owner = jnp.sum(
        jnp.where(named, slot_ref[...].astype(jnp.float32), 0.0), axis=1, keepdims=True
    )
    owner_block = jnp.broadcast_to(owner, (2, LANES)).astype(jnp.bfloat16)

    def message_copy(peer, source):
        return remote(
            message.at[peer], arrived.at[source], message_send.at[peer], message_recv.at[source], peer
        )

    for copy in cache_copies:
        copy.wait()
    positions = cache_ref.shape[1] * 2
    lane = lax.broadcasted_iota(jnp.int32, (HEADS_PER_GROUP, positions), 1)

    @pl.loop(0, KEY_HEADS)
    def _(head):
        heads = q_ref[
            :, pl.ds(pl.multiple_of(head * HEADS_PER_GROUP * HEAD_SIZE, 1024), HEADS_PER_GROUP * HEAD_SIZE)
        ].astype(jnp.float32)
        found = []
        for b in range(2):
            query = jnp.concatenate(
                [
                    heads[b : b + 1, g * HEAD_SIZE : (g + 1) * HEAD_SIZE]
                    for g in range(HEADS_PER_GROUP)
                ],
                axis=0,
            ).astype(jnp.bfloat16)
            pairs = cache[b, :, :, pl.ds(pl.multiple_of(head * HEAD_SIZE, HEAD_SIZE), HEAD_SIZE)].reshape(
                positions, HEAD_SIZE
            )
            scores = lax.dot_general(
                query, pairs, (((1,), (1,)), ((), ())), preferred_element_type=jnp.float32
            ) * (1.0 / math.sqrt(HEAD_SIZE))
            live = jnp.logical_and(lane < 2 * live_ref[b], lane % 2 == 0)
            scores = jnp.where(live, scores, masked_score)
            top = jnp.max(scores, axis=-1, keepdims=True)
            raw = jnp.where(live, jnp.exp(scores - top), 0.0)
            weights = raw / jnp.sum(raw, axis=-1, keepdims=True)
            weights = pltpu.roll(weights, 1, 1).astype(jnp.bfloat16)
            found.append(jnp.dot(weights, pairs, preferred_element_type=jnp.float32))
        for half in range(2):
            rows = [
                jnp.concatenate([f[half * 4 + g : half * 4 + g + 1] for g in range(4)], axis=1)
                for f in found
            ]
            peer = 2 * head + half
            message[peer, :, :depth] = jnp.concatenate(rows, axis=0).astype(jnp.bfloat16)
            message[peer, :, depth:] = owner_block

            @pl.when(peer != me)
            def _():
                message_copy(peer, me).start()

    arrived[me] = message[me]

    @pl.loop(1, count)
    def _(step):
        message_copy((me + step) % count, (me + step) % count).wait_recv()

    for source in range(count):
        z, y, c = source // 4, (source // 2) % 2, source % 2
        place = ((c * 2 + y) * 4 + z) * 2
        features[place : place + 2, :] = arrived[source].astype(jnp.float32)
    owners = features[:, depth : depth + 1]
    mine = features[:, :depth].astype(jnp.bfloat16)

    own_down.wait()

    @pl.loop(1, count)
    def _(step):
        down_copy((me + step) % count, (me + step) % count).wait_recv()

    rank = down_ref.shape[1]
    shrink_out[...] = lax.dot_general(
        down[...].reshape(count * rank, depth),
        mine,
        (((1,), (1,)), ((), ())),
        preferred_element_type=jnp.float32,
    ).reshape(count, rank, row_count)

    def shrink_copy(peer, source):
        return remote(
            shrink_out.at[peer], shrink_in.at[source], shrink_send.at[peer], shrink_recv.at[source], peer
        )

    @pl.loop(1, count)
    def _(step):
        shrink_copy((me + step) % count, me).start()

    shrink_in[me] = shrink_out[me]

    for j in range(CHUNKS):
        weight_copies[j].wait()
        part[j] = jnp.dot(mine, weight[j], preferred_element_type=jnp.float32).reshape(
            2, count, columns
        )

    @pl.loop(1, count)
    def _(step):
        shrink_copy((me + step) % count, (me + step) % count).wait_recv()

    shrink = jnp.sum(shrink_in[...], axis=0).astype(jnp.bfloat16)
    owned = owners == me.astype(jnp.float32)

    core_copies = [
        remote(part.at[j, 1 - my_core], core_in.at[j], core_send.at[j], core_recv.at[j], core_peer)
        for j in range(CHUNKS)
    ]
    y_copies = [
        remote(y_out.at[j, 1 - my_y], y_in.at[j], y_send.at[j], y_recv.at[j], y_peer)
        for j in range(CHUNKS)
    ]

    def z_copy(j, step):
        return remote(
            z_out.at[j, (my_z + step) % 4],
            z_in.at[j, step],
            z_send.at[j, step],
            z_recv.at[j, step],
            (me + 4 * step) % count,
        )

    for j in range(CHUNKS):
        delta = (
            adapter_scale
            * lax.dot_general(
                shrink,
                up_ref[0, :, j * columns : (j + 1) * columns],
                (((0,), (0,)), ((), ())),
                preferred_element_type=jnp.float32,
            )
        ).astype(jnp.bfloat16)
        delta = jnp.where(owned, delta.astype(jnp.float32), 0.0)
        part[j] = part[j] + delta.reshape(2, count, columns)
        core_copies[j].start()
    for j in range(CHUNKS):
        core_copies[j].wait_recv()
        chip_sum = part[j, my_core] + core_in[j]
        y_out[j] = chip_sum.reshape(2, count // 2, columns).astype(jnp.bfloat16)
        y_copies[j].start()
    for j in range(CHUNKS):
        y_copies[j].wait_recv()
        pair_sum = y_out[j, my_y].astype(jnp.float32) + y_in[j].astype(jnp.float32)
        for z in range(4):
            z_out[j, z] = pair_sum[2 * z : 2 * z + 2].astype(jnp.bfloat16)
        for step in range(1, 4):
            z_copy(j, step).start()
    square = jnp.zeros((2, 1), jnp.float32)
    for j in range(CHUNKS):
        here = slice(j * columns, (j + 1) * columns)
        value = residual_ref[:, here].astype(jnp.float32) + z_out[j, my_z].astype(jnp.float32)
        for step in range(1, 4):
            z_copy(j, step).wait_recv()
            value = value + z_in[j, step].astype(jnp.float32)
        total[:, here] = value
        hidden_ref[:, here] = value.astype(jnp.bfloat16)
        square = square + jnp.sum(value * value, axis=1, keepdims=True)
    scale = lax.rsqrt(square / weight_ref.shape[1] + norm_eps)
    normed_ref[...] = (total[...] * scale * gain_ref[...]).astype(jnp.bfloat16)

    @pl.loop(1, count)
    def _(step):
        peer = (me + step) % count
        message_copy(peer, me).wait_send()
        down_copy(peer, me).wait_send()
        shrink_copy(peer, me).wait_send()

    for j in range(CHUNKS):
        core_copies[j].wait_send()
        y_copies[j].wait_send()
        for step in range(1, 4):
            z_copy(j, step).wait_send()


def fused_call(
    queries,
    key_value_cache,
    live_cache_length,
    residual,
    row_adapter_index,
    adapter_slot_index,
    output_projection_weight,
    adapter_down_weight,
    adapter_up_weight,
    norm_gain_weight,
):
    count = lax.axis_size("tensor")
    depth, width = output_projection_weight.shape
    columns = width // CHUNKS
    rank = adapter_down_weight.shape[1]
    vmem = pl.BlockSpec(memory_space=pltpu.VMEM)
    hbm = pl.BlockSpec(memory_space=pl.ANY)
    smem = pl.BlockSpec(memory_space=pltpu.SMEM)
    dma = pltpu.SemaphoreType.DMA
    f32, bf16 = jnp.float32, jnp.bfloat16
    row = jax.ShapeDtypeStruct((2, width), bf16)
    return pl.pallas_call(
        functools.partial(fused, count, depth),
        out_shape=(row, row),
        in_specs=[vmem, hbm, smem, vmem, vmem, vmem, hbm, hbm, vmem, vmem],
        out_specs=(vmem, vmem),
        scratch_shapes=[
            pltpu.VMEM(key_value_cache.shape, bf16),
            pltpu.VMEM((CHUNKS, depth, columns), bf16),
            pltpu.VMEM((count, 2, depth + LANES), bf16),
            pltpu.VMEM((count, 2, depth + LANES), bf16),
            pltpu.VMEM((2 * count, depth + LANES), f32),
            pltpu.VMEM((count, rank, depth), bf16),
            pltpu.VMEM((count, rank, 2 * count), f32),
            pltpu.VMEM((count, rank, 2 * count), f32),
            pltpu.VMEM((CHUNKS, 2, count, columns), f32),
            pltpu.VMEM((CHUNKS, count, columns), f32),
            pltpu.VMEM((CHUNKS, 2, count // 2, columns), bf16),
            pltpu.VMEM((CHUNKS, count // 2, columns), bf16),
            pltpu.VMEM((CHUNKS, 4, 2, columns), bf16),
            pltpu.VMEM((CHUNKS, 4, 2, columns), bf16),
            pltpu.VMEM((2, width), f32),
            dma((2,)),
            dma((CHUNKS,)),
            dma((count,)),
            dma((count,)),
            dma((count,)),
            dma((count,)),
            dma((1,)),
            dma((count,)),
            dma((count,)),
            dma((CHUNKS,)),
            dma((CHUNKS,)),
            dma((CHUNKS,)),
            dma((CHUNKS,)),
            dma((CHUNKS, 4)),
            dma((CHUNKS, 4)),
        ],
        compiler_params=pltpu.CompilerParams(
            collective_id=0, has_side_effects=True, vmem_limit_bytes=48 * 1024 * 1024
        ),
    )(
        queries,
        key_value_cache,
        live_cache_length,
        residual,
        row_adapter_index,
        adapter_slot_index.reshape(1, -1),
        output_projection_weight,
        adapter_down_weight,
        adapter_up_weight,
        norm_gain_weight.reshape(1, -1),
    )


def solution(mesh):
    in_specs = (
        P(("groups", "tensor"), None),
        P(("groups", "tensor"), None, None, None),
        P(("groups", "tensor")),
        P(("groups", "tensor"), None),
        P(("groups", "tensor"), None),
        P(),
        P("tensor", None),
        P("tensor", None, None),
        P("tensor", None, None),
        P(),
    )
    out_specs = (P(("groups", "tensor"), None), P(("groups", "tensor"), None))
    body = fused_call if mesh.shape["tensor"] == 16 else shards
    return jax.shard_map(body, mesh=mesh, in_specs=in_specs, out_specs=out_specs, check_vma=False)
```

```python
import functools
import math

import jax
import jax.numpy as jnp
from jax import lax
from jax.experimental import pallas as pl
from jax.experimental.pallas import tpu as pltpu
from jax.sharding import PartitionSpec as P

HQ = 64
KEY_HEADS = 8
HEAD_SIZE = 128
HEADS_PER_GROUP = 8


adapter_scale = 2.0
norm_eps = 1e-05
masked_score = -1e30


def attend(queries, key_value_cache, live_cache_length):
    count_of_rows = queries.shape[0]
    cache_capacity = key_value_cache.shape[1]
    heads_of_query = queries.reshape(count_of_rows, KEY_HEADS, HEADS_PER_GROUP, HEAD_SIZE)
    block_of_keys = key_value_cache[:, :, 0, :].reshape(
        count_of_rows, cache_capacity, KEY_HEADS, HEAD_SIZE
    )
    block_of_values = key_value_cache[:, :, 1, :].reshape(
        count_of_rows, cache_capacity, KEY_HEADS, HEAD_SIZE
    )
    scores = jnp.einsum(
        "rhgd,rchd->rhgc", heads_of_query, block_of_keys, preferred_element_type=jnp.float32
    )
    scores = scores * (1.0 / math.sqrt(HEAD_SIZE))
    live_mask = (jnp.arange(cache_capacity, dtype=jnp.int32)[None, :] < live_cache_length[:, None])[
        :, None, None, :
    ]
    scores = jnp.where(live_mask, scores, masked_score)
    top_score = jnp.max(scores, axis=-1, keepdims=True)
    weights_raw = jnp.where(live_mask, jnp.exp(scores - top_score), 0.0)
    weights_low = (weights_raw / jnp.sum(weights_raw, axis=-1, keepdims=True)).astype(jnp.bfloat16)
    mixed = jnp.einsum(
        "rhgc,rchd->rhgd", weights_low, block_of_values, preferred_element_type=jnp.float32
    )
    return mixed.astype(jnp.bfloat16).reshape(count_of_rows, HQ * HEAD_SIZE)


def rows_to_shrink(tile_of_rows, selector, adapter_down_weight):
    shrink_factor = jnp.einsum(
        "dz,gz->dg", tile_of_rows, adapter_down_weight[0], preferred_element_type=jnp.float32
    )
    return (shrink_factor * selector).astype(jnp.bfloat16)


def shards(
    queries,
    key_value_cache,
    live_cache_length,
    residual,
    row_adapter_index,
    adapter_slot_index,
    output_projection_weight,
    adapter_down_weight,
    adapter_up_weight,
    norm_gain_weight,
):
    device_count = lax.axis_size("tensor")
    my_index = lax.axis_index("tensor")
    mixed = attend(queries, key_value_cache, live_cache_length)
    slot_hot = (
        row_adapter_index == jnp.arange(adapter_slot_index.shape[0], dtype=jnp.int32)[None, :]
    )
    owner_index = jnp.sum(jnp.where(slot_hot, adapter_slot_index[None, :], 0), axis=1)
    owner_hot = owner_index[:, None] == jnp.arange(device_count, dtype=jnp.int32)[None, :]
    gathered_rows, mark_rows = (
        lax.all_gather(mixed, "tensor", axis=0, tiled=True),
        lax.all_gather(owner_hot.astype(jnp.bfloat16), "tensor", axis=0, tiled=True),
    )
    owned_row_marks = lax.dynamic_slice_in_dim(mark_rows, my_index, 1, 1).astype(jnp.float32)
    width = output_projection_weight.shape[0]
    features = lax.dynamic_slice_in_dim(gathered_rows, my_index * width, width, 1)
    base_tile = jnp.dot(features, output_projection_weight, preferred_element_type=jnp.float32)
    shrink_factor = rows_to_shrink(gathered_rows, owned_row_marks, adapter_down_weight)
    delta_tile = (
        adapter_scale
        * jnp.dot(shrink_factor, adapter_up_weight[0], preferred_element_type=jnp.float32)
    ).astype(jnp.bfloat16)
    projected = lax.psum_scatter(
        base_tile + delta_tile.astype(jnp.float32), "tensor", scatter_dimension=0, tiled=True
    )
    hidden_sum = residual.astype(jnp.float32) + projected
    mean_square = jnp.mean(hidden_sum * hidden_sum, axis=-1, keepdims=True)
    normed = hidden_sum * lax.rsqrt(mean_square + norm_eps) * norm_gain_weight
    return (hidden_sum.astype(jnp.bfloat16), normed.astype(jnp.bfloat16))


CHUNKS = 4
LANES = 128


def remote(source, target, send_sem, recv_sem, peer):
    return pltpu.make_async_remote_copy(
        src_ref=source,
        dst_ref=target,
        send_sem=send_sem,
        recv_sem=recv_sem,
        device_id={"tensor": peer},
        device_id_type=pl.DeviceIdType.MESH,
    )


def fused(
    count,
    depth,
    q_hbm,
    cache_ref,
    live_hbm,
    residual_hbm,
    row_adapter_hbm,
    slot_hbm,
    weight_ref,
    down_ref,
    up_hbm,
    gain_hbm,
    hidden_ref,
    normed_ref,
    q_ref,
    live_ref,
    residual_ref,
    row_adapter_ref,
    slot_ref,
    up_ref,
    gain_ref,
    small_sem,
    cache,
    weight,
    message,
    arrived,
    features,
    down,
    shrink_out,
    shrink_in,
    part,
    core_in,
    y_out,
    y_in,
    z_out,
    z_in,
    total,
    cache_sem,
    weight_sem,
    message_send,
    message_recv,
    down_send,
    down_recv,
    down_local,
    shrink_send,
    shrink_recv,
    core_send,
    core_recv,
    y_send,
    y_recv,
    z_send,
    z_recv,
):
    me = lax.axis_index("tensor")
    my_core = me % 2
    my_y = (me // 2) % 2
    my_z = me // 4
    core_peer = me + 1 - 2 * my_core
    y_peer = me + 2 - 4 * my_y
    row_count = 2 * count
    columns = weight_ref.shape[1] // CHUNKS

    cache_copies = [
        pltpu.make_async_copy(cache_ref.at[b], cache.at[b], cache_sem.at[b]) for b in range(2)
    ]
    weight_copies = [
        pltpu.make_async_copy(
            weight_ref.at[:, pl.ds(j * columns, columns)], weight.at[j], weight_sem.at[j]
        )
        for j in range(CHUNKS)
    ]
    early = [(q_hbm, q_ref), (live_hbm, live_ref), (row_adapter_hbm, row_adapter_ref), (slot_hbm, slot_ref)]
    late = [(up_hbm, up_ref), (residual_hbm, residual_ref), (gain_hbm, gain_ref)]
    small_copies = [
        pltpu.make_async_copy(source, target, small_sem.at[i])
        for i, (source, target) in enumerate(early + late)
    ]
    for copy in small_copies[: len(early)] + cache_copies + weight_copies + small_copies[len(early) :]:
        copy.start()

    barrier = pltpu.get_barrier_semaphore()

    @pl.loop(1, count)
    def _(step):
        pl.semaphore_signal(
            barrier,
            inc=1,
            device_id={"tensor": (me + step) % count},
            device_id_type=pl.DeviceIdType.MESH,
        )

    pl.semaphore_wait(barrier, count - 1)

    def down_copy(peer, source):
        return remote(
            down_ref.at[0, :, pl.ds(pl.multiple_of(peer * depth, depth), depth)],
            down.at[source],
            down_send.at[peer],
            down_recv.at[source],
            peer,
        )

    @pl.loop(1, count)
    def _(step):
        down_copy((me + step) % count, me).start()

    own_down = pltpu.make_async_copy(
        down_ref.at[0, :, pl.ds(pl.multiple_of(me * depth, depth), depth)],
        down.at[me],
        down_local.at[0],
    )
    own_down.start()

    for copy in small_copies[: len(early)]:
        copy.wait()
    adapters = slot_ref.shape[1]
    row_adapter = jnp.where(
        lax.broadcasted_iota(jnp.int32, (2, adapters), 0) == 0, row_adapter_ref[0], row_adapter_ref[1]
    )
    named = lax.broadcasted_iota(jnp.int32, (2, adapters), 1) == row_adapter
    owner = jnp.sum(
        jnp.where(named, slot_ref[...].astype(jnp.float32), 0.0), axis=1, keepdims=True
    )
    owner_block = jnp.broadcast_to(owner, (2, LANES)).astype(jnp.bfloat16)

    def message_copy(peer, source):
        return remote(
            message.at[peer], arrived.at[source], message_send.at[peer], message_recv.at[source], peer
        )

    for copy in cache_copies:
        copy.wait()
    positions = cache_ref.shape[1] * 2
    lane = lax.broadcasted_iota(jnp.int32, (HEADS_PER_GROUP, positions), 1)

    @pl.loop(0, KEY_HEADS)
    def _(head):
        heads = q_ref[
            :, pl.ds(pl.multiple_of(head * HEADS_PER_GROUP * HEAD_SIZE, 1024), HEADS_PER_GROUP * HEAD_SIZE)
        ].astype(jnp.float32)
        found = []
        for b in range(2):
            query = jnp.concatenate(
                [
                    heads[b : b + 1, g * HEAD_SIZE : (g + 1) * HEAD_SIZE]
                    for g in range(HEADS_PER_GROUP)
                ],
                axis=0,
            ).astype(jnp.bfloat16)
            pairs = cache[b, :, :, pl.ds(pl.multiple_of(head * HEAD_SIZE, HEAD_SIZE), HEAD_SIZE)].reshape(
                positions, HEAD_SIZE
            )
            scores = lax.dot_general(
                query, pairs, (((1,), (1,)), ((), ())), preferred_element_type=jnp.float32
            ) * (1.0 / math.sqrt(HEAD_SIZE))
            live = jnp.logical_and(lane < 2 * live_ref[b], lane % 2 == 0)
            scores = jnp.where(live, scores, masked_score)
            top = jnp.max(scores, axis=-1, keepdims=True)
            raw = jnp.where(live, jnp.exp(scores - top), 0.0)
            weights = raw / jnp.sum(raw, axis=-1, keepdims=True)
            weights = pltpu.roll(weights, 1, 1).astype(jnp.bfloat16)
            found.append(jnp.dot(weights, pairs, preferred_element_type=jnp.float32))
        for half in range(2):
            rows = [
                jnp.concatenate([f[half * 4 + g : half * 4 + g + 1] for g in range(4)], axis=1)
                for f in found
            ]
            peer = 2 * head + half
            message[peer, :, :depth] = jnp.concatenate(rows, axis=0).astype(jnp.bfloat16)
            message[peer, :, depth:] = owner_block

            @pl.when(peer != me)
            def _():
                message_copy(peer, me).start()

    arrived[me] = message[me]

    @pl.loop(1, count)
    def _(step):
        message_copy((me + step) % count, (me + step) % count).wait_recv()

    for source in range(count):
        z, y, c = source // 4, (source // 2) % 2, source % 2
        place = ((c * 2 + y) * 4 + z) * 2
        features[place : place + 2, :] = arrived[source].astype(jnp.float32)
    owners = features[:, depth : depth + 1]
    mine = features[:, :depth].astype(jnp.bfloat16)

    own_down.wait()

    @pl.loop(1, count)
    def _(step):
        down_copy((me + step) % count, (me + step) % count).wait_recv()

    rank = down_ref.shape[1]
    shrink_out[...] = lax.dot_general(
        down[...].reshape(count * rank, depth),
        mine,
        (((1,), (1,)), ((), ())),
        preferred_element_type=jnp.float32,
    ).reshape(count, rank, row_count)

    def shrink_copy(peer, source):
        return remote(
            shrink_out.at[peer], shrink_in.at[source], shrink_send.at[peer], shrink_recv.at[source], peer
        )

    @pl.loop(1, count)
    def _(step):
        shrink_copy((me + step) % count, me).start()

    shrink_in[me] = shrink_out[me]

    for j in range(CHUNKS):
        weight_copies[j].wait()
        part[j] = jnp.dot(mine, weight[j], preferred_element_type=jnp.float32).reshape(
            2, count, columns
        )

    @pl.loop(1, count)
    def _(step):
        shrink_copy((me + step) % count, (me + step) % count).wait_recv()

    for copy in small_copies[len(early) :]:
        copy.wait()
    shrink = jnp.sum(shrink_in[...], axis=0).astype(jnp.bfloat16)
    owned = owners == me.astype(jnp.float32)

    core_copies = [
        remote(part.at[j, 1 - my_core], core_in.at[j], core_send.at[j], core_recv.at[j], core_peer)
        for j in range(CHUNKS)
    ]
    y_copies = [
        remote(y_out.at[j, 1 - my_y], y_in.at[j], y_send.at[j], y_recv.at[j], y_peer)
        for j in range(CHUNKS)
    ]

    def z_copy(j, step):
        return remote(
            z_out.at[j, (my_z + step) % 4],
            z_in.at[j, step],
            z_send.at[j, step],
            z_recv.at[j, step],
            (me + 4 * step) % count,
        )

    for j in range(CHUNKS):
        delta = (
            adapter_scale
            * lax.dot_general(
                shrink,
                up_ref[0, :, j * columns : (j + 1) * columns],
                (((0,), (0,)), ((), ())),
                preferred_element_type=jnp.float32,
            )
        ).astype(jnp.bfloat16)
        delta = jnp.where(owned, delta.astype(jnp.float32), 0.0)
        part[j] = part[j] + delta.reshape(2, count, columns)
        core_copies[j].start()
    for j in range(CHUNKS):
        core_copies[j].wait_recv()
        chip_sum = part[j, my_core] + core_in[j]
        y_out[j] = chip_sum.reshape(2, count // 2, columns).astype(jnp.bfloat16)
        y_copies[j].start()
    for j in range(CHUNKS):
        y_copies[j].wait_recv()
        pair_sum = y_out[j, my_y].astype(jnp.float32) + y_in[j].astype(jnp.float32)
        for z in range(4):
            z_out[j, z] = pair_sum[2 * z : 2 * z + 2].astype(jnp.bfloat16)
        for step in range(1, 4):
            z_copy(j, step).start()
    square = jnp.zeros((2, 1), jnp.float32)
    for j in range(CHUNKS):
        here = slice(j * columns, (j + 1) * columns)
        value = residual_ref[:, here].astype(jnp.float32) + z_out[j, my_z].astype(jnp.float32)
        for step in range(1, 4):
            z_copy(j, step).wait_recv()
            value = value + z_in[j, step].astype(jnp.float32)
        total[:, here] = value
        hidden_ref[:, here] = value.astype(jnp.bfloat16)
        square = square + jnp.sum(value * value, axis=1, keepdims=True)
    scale = lax.rsqrt(square / weight_ref.shape[1] + norm_eps)
    normed_ref[...] = (total[...] * scale * gain_ref[...]).astype(jnp.bfloat16)

    @pl.loop(1, count)
    def _(step):
        peer = (me + step) % count
        message_copy(peer, me).wait_send()
        down_copy(peer, me).wait_send()
        shrink_copy(peer, me).wait_send()

    for j in range(CHUNKS):
        core_copies[j].wait_send()
        y_copies[j].wait_send()
        for step in range(1, 4):
            z_copy(j, step).wait_send()


def fused_call(
    queries,
    key_value_cache,
    live_cache_length,
    residual,
    row_adapter_index,
    adapter_slot_index,
    output_projection_weight,
    adapter_down_weight,
    adapter_up_weight,
    norm_gain_weight,
):
    count = lax.axis_size("tensor")
    depth, width = output_projection_weight.shape
    columns = width // CHUNKS
    rank = adapter_down_weight.shape[1]
    vmem = pl.BlockSpec(memory_space=pltpu.VMEM)
    hbm = pl.BlockSpec(memory_space=pl.ANY)
    dma = pltpu.SemaphoreType.DMA
    f32, bf16 = jnp.float32, jnp.bfloat16
    row = jax.ShapeDtypeStruct((2, width), bf16)
    return pl.pallas_call(
        functools.partial(fused, count, depth),
        out_shape=(row, row),
        in_specs=[hbm] * 10,
        out_specs=(vmem, vmem),
        scratch_shapes=[
            pltpu.VMEM(queries.shape, bf16),
            pltpu.SMEM(live_cache_length.shape, jnp.int32),
            pltpu.VMEM(residual.shape, bf16),
            pltpu.SMEM(live_cache_length.shape, jnp.int32),
            pltpu.VMEM((1, adapter_slot_index.shape[0]), jnp.int32),
            pltpu.VMEM(adapter_up_weight.shape, bf16),
            pltpu.VMEM((1, width), f32),
            dma((7,)),
            pltpu.VMEM(key_value_cache.shape, bf16),
            pltpu.VMEM((CHUNKS, depth, columns), bf16),
            pltpu.VMEM((count, 2, depth + LANES), bf16),
            pltpu.VMEM((count, 2, depth + LANES), bf16),
            pltpu.VMEM((2 * count, depth + LANES), f32),
            pltpu.VMEM((count, rank, depth), bf16),
            pltpu.VMEM((count, rank, 2 * count), f32),
            pltpu.VMEM((count, rank, 2 * count), f32),
            pltpu.VMEM((CHUNKS, 2, count, columns), f32),
            pltpu.VMEM((CHUNKS, count, columns), f32),
            pltpu.VMEM((CHUNKS, 2, count // 2, columns), bf16),
            pltpu.VMEM((CHUNKS, count // 2, columns), bf16),
            pltpu.VMEM((CHUNKS, 4, 2, columns), bf16),
            pltpu.VMEM((CHUNKS, 4, 2, columns), bf16),
            pltpu.VMEM((2, width), f32),
            dma((2,)),
            dma((CHUNKS,)),
            dma((count,)),
            dma((count,)),
            dma((count,)),
            dma((count,)),
            dma((1,)),
            dma((count,)),
            dma((count,)),
            dma((CHUNKS,)),
            dma((CHUNKS,)),
            dma((CHUNKS,)),
            dma((CHUNKS,)),
            dma((CHUNKS, 4)),
            dma((CHUNKS, 4)),
        ],
        compiler_params=pltpu.CompilerParams(
            collective_id=0, has_side_effects=True, vmem_limit_bytes=60 * 1024 * 1024
        ),
    )(
        queries,
        key_value_cache,
        live_cache_length,
        residual,
        row_adapter_index.reshape(-1),
        adapter_slot_index.reshape(1, -1),
        output_projection_weight,
        adapter_down_weight,
        adapter_up_weight,
        norm_gain_weight.reshape(1, -1),
    )


def solution(mesh):
    in_specs = (
        P(("groups", "tensor"), None),
        P(("groups", "tensor"), None, None, None),
        P(("groups", "tensor")),
        P(("groups", "tensor"), None),
        P(("groups", "tensor"), None),
        P(),
        P("tensor", None),
        P("tensor", None, None),
        P("tensor", None, None),
        P(),
    )
    out_specs = (P(("groups", "tensor"), None), P(("groups", "tensor"), None))
    body = fused_call if mesh.shape["tensor"] == 16 else shards
    return jax.shard_map(body, mesh=mesh, in_specs=in_specs, out_specs=out_specs, check_vma=False)
```

```python
import functools
import math

import jax
import jax.numpy as jnp
from jax import lax
from jax.experimental import pallas as pl
from jax.experimental.pallas import tpu as pltpu
from jax.sharding import PartitionSpec as P

HQ = 64
KEY_HEADS = 8
HEAD_SIZE = 128
HEADS_PER_GROUP = 8


adapter_scale = 2.0
norm_eps = 1e-05
masked_score = -1e30


def attend(queries, key_value_cache, live_cache_length):
    count_of_rows = queries.shape[0]
    cache_capacity = key_value_cache.shape[1]
    heads_of_query = queries.reshape(count_of_rows, KEY_HEADS, HEADS_PER_GROUP, HEAD_SIZE)
    block_of_keys = key_value_cache[:, :, 0, :].reshape(
        count_of_rows, cache_capacity, KEY_HEADS, HEAD_SIZE
    )
    block_of_values = key_value_cache[:, :, 1, :].reshape(
        count_of_rows, cache_capacity, KEY_HEADS, HEAD_SIZE
    )
    scores = jnp.einsum(
        "rhgd,rchd->rhgc", heads_of_query, block_of_keys, preferred_element_type=jnp.float32
    )
    scores = scores * (1.0 / math.sqrt(HEAD_SIZE))
    live_mask = (jnp.arange(cache_capacity, dtype=jnp.int32)[None, :] < live_cache_length[:, None])[
        :, None, None, :
    ]
    scores = jnp.where(live_mask, scores, masked_score)
    top_score = jnp.max(scores, axis=-1, keepdims=True)
    weights_raw = jnp.where(live_mask, jnp.exp(scores - top_score), 0.0)
    weights_low = (weights_raw / jnp.sum(weights_raw, axis=-1, keepdims=True)).astype(jnp.bfloat16)
    mixed = jnp.einsum(
        "rhgc,rchd->rhgd", weights_low, block_of_values, preferred_element_type=jnp.float32
    )
    return mixed.astype(jnp.bfloat16).reshape(count_of_rows, HQ * HEAD_SIZE)


def rows_to_shrink(tile_of_rows, selector, adapter_down_weight):
    shrink_factor = jnp.einsum(
        "dz,gz->dg", tile_of_rows, adapter_down_weight[0], preferred_element_type=jnp.float32
    )
    return (shrink_factor * selector).astype(jnp.bfloat16)


def shards(
    queries,
    key_value_cache,
    live_cache_length,
    residual,
    row_adapter_index,
    adapter_slot_index,
    output_projection_weight,
    adapter_down_weight,
    adapter_up_weight,
    norm_gain_weight,
):
    device_count = lax.axis_size("tensor")
    my_index = lax.axis_index("tensor")
    mixed = attend(queries, key_value_cache, live_cache_length)
    slot_hot = (
        row_adapter_index == jnp.arange(adapter_slot_index.shape[0], dtype=jnp.int32)[None, :]
    )
    owner_index = jnp.sum(jnp.where(slot_hot, adapter_slot_index[None, :], 0), axis=1)
    owner_hot = owner_index[:, None] == jnp.arange(device_count, dtype=jnp.int32)[None, :]
    gathered_rows, mark_rows = (
        lax.all_gather(mixed, "tensor", axis=0, tiled=True),
        lax.all_gather(owner_hot.astype(jnp.bfloat16), "tensor", axis=0, tiled=True),
    )
    owned_row_marks = lax.dynamic_slice_in_dim(mark_rows, my_index, 1, 1).astype(jnp.float32)
    width = output_projection_weight.shape[0]
    features = lax.dynamic_slice_in_dim(gathered_rows, my_index * width, width, 1)
    base_tile = jnp.dot(features, output_projection_weight, preferred_element_type=jnp.float32)
    shrink_factor = rows_to_shrink(gathered_rows, owned_row_marks, adapter_down_weight)
    delta_tile = (
        adapter_scale
        * jnp.dot(shrink_factor, adapter_up_weight[0], preferred_element_type=jnp.float32)
    ).astype(jnp.bfloat16)
    projected = lax.psum_scatter(
        base_tile + delta_tile.astype(jnp.float32), "tensor", scatter_dimension=0, tiled=True
    )
    hidden_sum = residual.astype(jnp.float32) + projected
    mean_square = jnp.mean(hidden_sum * hidden_sum, axis=-1, keepdims=True)
    normed = hidden_sum * lax.rsqrt(mean_square + norm_eps) * norm_gain_weight
    return (hidden_sum.astype(jnp.bfloat16), normed.astype(jnp.bfloat16))


CHUNKS = 4
LAG_Y = 4
LAG_Z = 8
LANES = 128


def remote(source, target, send_sem, recv_sem, peer):
    return pltpu.make_async_remote_copy(
        src_ref=source,
        dst_ref=target,
        send_sem=send_sem,
        recv_sem=recv_sem,
        device_id={"tensor": peer},
        device_id_type=pl.DeviceIdType.MESH,
    )


def fused(
    count,
    depth,
    q_hbm,
    cache_ref,
    live_hbm,
    residual_hbm,
    row_adapter_hbm,
    slot_hbm,
    weight_ref,
    down_ref,
    up_hbm,
    gain_hbm,
    hidden_ref,
    normed_ref,
    q_ref,
    live_ref,
    residual_ref,
    row_adapter_ref,
    slot_ref,
    up_ref,
    gain_ref,
    small_sem,
    cache,
    weight,
    message,
    arrived,
    features,
    down,
    shrink_out,
    shrink_in,
    part,
    core_out,
    core_in,
    y_out,
    y_in,
    z_out,
    z_in,
    total,
    cache_sem,
    weight_sem,
    message_send,
    message_recv,
    down_send,
    down_recv,
    down_local,
    shrink_send,
    shrink_recv,
    core_send,
    core_recv,
    y_send,
    y_recv,
    z_send,
    z_recv,
):
    me = lax.axis_index("tensor")
    my_core = me % 2
    my_y = (me // 2) % 2
    my_z = me // 4
    core_peer = me + 1 - 2 * my_core
    y_peer = me + 2 - 4 * my_y
    row_count = 2 * count
    columns = weight_ref.shape[1] // CHUNKS

    cache_copies = [
        pltpu.make_async_copy(cache_ref.at[b], cache.at[b], cache_sem.at[b]) for b in range(2)
    ]
    weight_copies = [
        pltpu.make_async_copy(
            weight_ref.at[:, pl.ds(j * columns, columns)], weight.at[j], weight_sem.at[j]
        )
        for j in range(CHUNKS)
    ]
    early = [(q_hbm, q_ref), (live_hbm, live_ref), (row_adapter_hbm, row_adapter_ref), (slot_hbm, slot_ref)]
    late = [(up_hbm, up_ref), (residual_hbm, residual_ref), (gain_hbm, gain_ref)]
    small_copies = [
        pltpu.make_async_copy(source, target, small_sem.at[i])
        for i, (source, target) in enumerate(early + late)
    ]
    for copy in small_copies[: len(early)] + cache_copies + weight_copies + small_copies[len(early) :]:
        copy.start()

    barrier = pltpu.get_barrier_semaphore()

    @pl.loop(1, count)
    def _(step):
        pl.semaphore_signal(
            barrier,
            inc=1,
            device_id={"tensor": (me + step) % count},
            device_id_type=pl.DeviceIdType.MESH,
        )

    pl.semaphore_wait(barrier, count - 1)

    def down_copy(peer, source):
        return remote(
            down_ref.at[0, :, pl.ds(pl.multiple_of(peer * depth, depth), depth)],
            down.at[source],
            down_send.at[peer],
            down_recv.at[source],
            peer,
        )

    @pl.loop(1, count)
    def _(step):
        down_copy((me + step) % count, me).start()

    own_down = pltpu.make_async_copy(
        down_ref.at[0, :, pl.ds(pl.multiple_of(me * depth, depth), depth)],
        down.at[me],
        down_local.at[0],
    )
    own_down.start()

    for copy in small_copies[: len(early)]:
        copy.wait()
    adapters = slot_ref.shape[1]
    row_adapter = jnp.where(
        lax.broadcasted_iota(jnp.int32, (2, adapters), 0) == 0, row_adapter_ref[0], row_adapter_ref[1]
    )
    named = lax.broadcasted_iota(jnp.int32, (2, adapters), 1) == row_adapter
    owner = jnp.sum(
        jnp.where(named, slot_ref[...].astype(jnp.float32), 0.0), axis=1, keepdims=True
    )
    owner_block = jnp.broadcast_to(owner, (2, LANES)).astype(jnp.bfloat16)

    def message_copy(peer, source):
        return remote(
            message.at[peer], arrived.at[source], message_send.at[peer], message_recv.at[source], peer
        )

    for copy in cache_copies:
        copy.wait()
    positions = cache_ref.shape[1] * 2
    lane = lax.broadcasted_iota(jnp.int32, (HEADS_PER_GROUP, positions), 1)

    @pl.loop(0, KEY_HEADS)
    def _(head):
        heads = q_ref[
            :, pl.ds(pl.multiple_of(head * HEADS_PER_GROUP * HEAD_SIZE, 1024), HEADS_PER_GROUP * HEAD_SIZE)
        ].astype(jnp.float32)
        found = []
        for b in range(2):
            query = jnp.concatenate(
                [
                    heads[b : b + 1, g * HEAD_SIZE : (g + 1) * HEAD_SIZE]
                    for g in range(HEADS_PER_GROUP)
                ],
                axis=0,
            ).astype(jnp.bfloat16)
            pairs = cache[b, :, :, pl.ds(pl.multiple_of(head * HEAD_SIZE, HEAD_SIZE), HEAD_SIZE)].reshape(
                positions, HEAD_SIZE
            )
            scores = lax.dot_general(
                query, pairs, (((1,), (1,)), ((), ())), preferred_element_type=jnp.float32
            ) * (1.0 / math.sqrt(HEAD_SIZE))
            live = jnp.logical_and(lane < 2 * live_ref[b], lane % 2 == 0)
            scores = jnp.where(live, scores, masked_score)
            top = jnp.max(scores, axis=-1, keepdims=True)
            raw = jnp.where(live, jnp.exp(scores - top), 0.0)
            weights = raw / jnp.sum(raw, axis=-1, keepdims=True)
            weights = pltpu.roll(weights, 1, 1).astype(jnp.bfloat16)
            found.append(jnp.dot(weights, pairs, preferred_element_type=jnp.float32))
        for half in range(2):
            rows = [
                jnp.concatenate([f[half * 4 + g : half * 4 + g + 1] for g in range(4)], axis=1)
                for f in found
            ]
            peer = 2 * head + half
            message[peer, :, :depth] = jnp.concatenate(rows, axis=0).astype(jnp.bfloat16)
            message[peer, :, depth:] = owner_block

            @pl.when(peer != me)
            def _():
                message_copy(peer, me).start()

    arrived[me] = message[me]

    @pl.loop(1, count)
    def _(step):
        message_copy((me + step) % count, (me + step) % count).wait_recv()

    for source in range(count):
        z, y, c = source // 4, (source // 2) % 2, source % 2
        place = ((c * 2 + y) * 4 + z) * 2
        features[place : place + 2, :] = arrived[source].astype(jnp.float32)
    owners = features[:, depth : depth + 1]
    mine = features[:, :depth].astype(jnp.bfloat16)

    own_down.wait()

    @pl.loop(1, count)
    def _(step):
        down_copy((me + step) % count, (me + step) % count).wait_recv()

    rank = down_ref.shape[1]
    shrink_out[...] = lax.dot_general(
        down[...].reshape(count * rank, depth),
        mine,
        (((1,), (1,)), ((), ())),
        preferred_element_type=jnp.float32,
    ).reshape(count, rank, row_count).astype(jnp.bfloat16)

    def shrink_copy(peer, source):
        return remote(
            shrink_out.at[peer], shrink_in.at[source], shrink_send.at[peer], shrink_recv.at[source], peer
        )

    @pl.loop(1, count)
    def _(step):
        shrink_copy((me + step) % count, me).start()

    shrink_in[me] = shrink_out[me]

    for j in range(CHUNKS):
        weight_copies[j].wait()
        part[j] = jnp.dot(mine, weight[j], preferred_element_type=jnp.float32).reshape(
            2, count, columns
        )

    @pl.loop(1, count)
    def _(step):
        shrink_copy((me + step) % count, (me + step) % count).wait_recv()

    for copy in small_copies[len(early) :]:
        copy.wait()
    shrink = jnp.sum(shrink_in[...].astype(jnp.float32), axis=0).astype(jnp.bfloat16)
    owned = owners == me.astype(jnp.float32)

    core_copies = [
        remote(core_out.at[j], core_in.at[j], core_send.at[j], core_recv.at[j], core_peer)
        for j in range(CHUNKS)
    ]
    y_copies = [
        remote(y_out.at[j, 1 - my_y], y_in.at[j], y_send.at[j], y_recv.at[j], y_peer)
        for j in range(CHUNKS)
    ]

    def z_copy(j, step):
        return remote(
            z_out.at[j, (my_z + step) % 4],
            z_in.at[j, step],
            z_send.at[j, step],
            z_recv.at[j, step],
            (me + 4 * step) % count,
        )

    def send_to_core(j):
        delta = (
            adapter_scale
            * lax.dot_general(
                shrink,
                up_ref[0, :, j * columns : (j + 1) * columns],
                (((0,), (0,)), ((), ())),
                preferred_element_type=jnp.float32,
            )
        ).astype(jnp.bfloat16)
        delta = jnp.where(owned, delta.astype(jnp.float32), 0.0)
        part[j] = part[j] + delta.reshape(2, count, columns)
        core_out[j] = part[j, 1 - my_core].astype(jnp.bfloat16)
        core_copies[j].start()

    def send_along_y(j):
        core_copies[j].wait_recv()
        chip_sum = part[j, my_core] + core_in[j].astype(jnp.float32)
        y_out[j] = chip_sum.reshape(2, count // 2, columns).astype(jnp.bfloat16)
        y_copies[j].start()

    def send_along_z(j):
        y_copies[j].wait_recv()
        pair_sum = y_out[j, my_y].astype(jnp.float32) + y_in[j].astype(jnp.float32)
        for z in range(4):
            z_out[j, z] = pair_sum[2 * z : 2 * z + 2].astype(jnp.bfloat16)
        for step in range(1, 4):
            z_copy(j, step).start()

    for step in range(CHUNKS + LAG_Z):
        if step < CHUNKS:
            send_to_core(step)
        if 0 <= step - LAG_Y < CHUNKS:
            send_along_y(step - LAG_Y)
        if 0 <= step - LAG_Z < CHUNKS:
            send_along_z(step - LAG_Z)
    square = jnp.zeros((2, 1), jnp.float32)
    for j in range(CHUNKS):
        here = slice(j * columns, (j + 1) * columns)
        value = residual_ref[:, here].astype(jnp.float32) + z_out[j, my_z].astype(jnp.float32)
        for step in range(1, 4):
            z_copy(j, step).wait_recv()
            value = value + z_in[j, step].astype(jnp.float32)
        total[:, here] = value
        hidden_ref[:, here] = value.astype(jnp.bfloat16)
        square = square + jnp.sum(value * value, axis=1, keepdims=True)
    scale = lax.rsqrt(square / weight_ref.shape[1] + norm_eps)
    normed_ref[...] = (total[...] * scale * gain_ref[...]).astype(jnp.bfloat16)

    @pl.loop(1, count)
    def _(step):
        peer = (me + step) % count
        message_copy(peer, me).wait_send()
        down_copy(peer, me).wait_send()
        shrink_copy(peer, me).wait_send()

    for j in range(CHUNKS):
        core_copies[j].wait_send()
        y_copies[j].wait_send()
        for step in range(1, 4):
            z_copy(j, step).wait_send()


def fused_call(
    queries,
    key_value_cache,
    live_cache_length,
    residual,
    row_adapter_index,
    adapter_slot_index,
    output_projection_weight,
    adapter_down_weight,
    adapter_up_weight,
    norm_gain_weight,
):
    count = lax.axis_size("tensor")
    depth, width = output_projection_weight.shape
    columns = width // CHUNKS
    rank = adapter_down_weight.shape[1]
    vmem = pl.BlockSpec(memory_space=pltpu.VMEM)
    hbm = pl.BlockSpec(memory_space=pl.ANY)
    dma = pltpu.SemaphoreType.DMA
    f32, bf16 = jnp.float32, jnp.bfloat16
    row = jax.ShapeDtypeStruct((2, width), bf16)
    return pl.pallas_call(
        functools.partial(fused, count, depth),
        out_shape=(row, row),
        in_specs=[hbm] * 10,
        out_specs=(vmem, vmem),
        scratch_shapes=[
            pltpu.VMEM(queries.shape, bf16),
            pltpu.SMEM(live_cache_length.shape, jnp.int32),
            pltpu.VMEM(residual.shape, bf16),
            pltpu.SMEM(live_cache_length.shape, jnp.int32),
            pltpu.VMEM((1, adapter_slot_index.shape[0]), jnp.int32),
            pltpu.VMEM(adapter_up_weight.shape, bf16),
            pltpu.VMEM((1, width), f32),
            dma((7,)),
            pltpu.VMEM(key_value_cache.shape, bf16),
            pltpu.VMEM((CHUNKS, depth, columns), bf16),
            pltpu.VMEM((count, 2, depth + LANES), bf16),
            pltpu.VMEM((count, 2, depth + LANES), bf16),
            pltpu.VMEM((2 * count, depth + LANES), f32),
            pltpu.VMEM((count, rank, depth), bf16),
            pltpu.VMEM((count, rank, 2 * count), bf16),
            pltpu.VMEM((count, rank, 2 * count), bf16),
            pltpu.VMEM((CHUNKS, 2, count, columns), f32),
            pltpu.VMEM((CHUNKS, count, columns), bf16),
            pltpu.VMEM((CHUNKS, count, columns), bf16),
            pltpu.VMEM((CHUNKS, 2, count // 2, columns), bf16),
            pltpu.VMEM((CHUNKS, count // 2, columns), bf16),
            pltpu.VMEM((CHUNKS, 4, 2, columns), bf16),
            pltpu.VMEM((CHUNKS, 4, 2, columns), bf16),
            pltpu.VMEM((2, width), f32),
            dma((2,)),
            dma((CHUNKS,)),
            dma((count,)),
            dma((count,)),
            dma((count,)),
            dma((count,)),
            dma((1,)),
            dma((count,)),
            dma((count,)),
            dma((CHUNKS,)),
            dma((CHUNKS,)),
            dma((CHUNKS,)),
            dma((CHUNKS,)),
            dma((CHUNKS, 4)),
            dma((CHUNKS, 4)),
        ],
        compiler_params=pltpu.CompilerParams(
            collective_id=0, has_side_effects=True, vmem_limit_bytes=60 * 1024 * 1024
        ),
    )(
        queries,
        key_value_cache,
        live_cache_length,
        residual,
        row_adapter_index.reshape(-1),
        adapter_slot_index.reshape(1, -1),
        output_projection_weight,
        adapter_down_weight,
        adapter_up_weight,
        norm_gain_weight.reshape(1, -1),
    )


def solution(mesh):
    in_specs = (
        P(("groups", "tensor"), None),
        P(("groups", "tensor"), None, None, None),
        P(("groups", "tensor")),
        P(("groups", "tensor"), None),
        P(("groups", "tensor"), None),
        P(),
        P("tensor", None),
        P("tensor", None, None),
        P("tensor", None, None),
        P(),
    )
    out_specs = (P(("groups", "tensor"), None), P(("groups", "tensor"), None))
    body = fused_call if mesh.shape["tensor"] == 16 else shards
    return jax.shard_map(body, mesh=mesh, in_specs=in_specs, out_specs=out_specs, check_vma=False)
```
